256 devices in a mesh: ctx: 32 (over x, y, core), head: 8 (over z).
Axes of the slice: x: 4, y: 4, z: 8, core: 2. Of those that a mesh axis runs over, the one named last changes fastest.
Arguments:
- queries: bfloat16 [6144, 8192], P('ctx', 'head'), may hold values from -200 to 200
- key_states: bfloat16 [6144, 1024], P('ctx', 'head'), may hold values from -8 to 8
- value_states: bfloat16 [6144, 1024], P('ctx', 'head'), may hold values from -6 to 6
- head_gates: float32 [64], P('head'), may hold values from 0.1 to 1
- retrieval: int32 [64], P('head'), may hold values 0 or 1
- sink_count: int32 [64], P('head'), may hold values from 1 to 128, as said below
- window_len: int32 [64], P('head'), may hold values from 1024 to 2048, as said below
- out_grad: bfloat16 [6144, 8192], P('ctx', 'head'), may hold values from -6 to 6
Outputs:
- attended: bfloat16 [6144, 8192], P('ctx', 'head')
- grad_queries: bfloat16 [6144, 8192], P('ctx', 'head')
- grad_keys: bfloat16 [6144, 1024], P('ctx', 'head')
- grad_values: bfloat16 [6144, 1024], P('ctx', 'head')
- grad_gates: float32 [64], replicated
The draws below stay inside these ranges and needn't reach their ends.
Inputs may be any that keep to these rules, and one draw needn't show every extreme that they name: `sink_count`: number of sink tokens of each head; some head has exactly 128 and some head exactly 1. `window_len`: window of each head; some head has exactly 2048 and some head exactly half of 2048.
All inputs are finite; a program needn't handle non-finite values. No bound on the sum of `retrieval` on one device may be relied on, other than what follows from the above.
Results may differ from the reference program's by a relative error of at most 0.04.
Values may be sent and summed in bfloat16 or wider, within the bound.
A program may use at most 128 MiB of HBM per device.

```python
import jax
import jax.numpy as jnp
from jax import lax

HQ = 64
HK = 8
DH = 128
SINKS = 128
WINDOW = 2048
TOKENS = 6144


def shared_keys(key):
    return jax.random.normal(key, (TOKENS, HK, DH), jnp.float32)


def draw_queries(key, part):
    key = jax.random.fold_in(key, 2)
    result = jax.random.normal(key, (TOKENS, HQ, DH), jnp.float32) * 1.5
    return result.reshape(TOKENS, HQ * DH).astype(jnp.bfloat16)


def draw_key_states(key, part):
    base = shared_keys(key)
    result = base
    return result.reshape(TOKENS, HK * DH).astype(jnp.bfloat16)


def draw_sink_count(key, part):
    key = jax.random.fold_in(key, 21)
    counts = jax.random.randint(key, (HQ,), 1, SINKS + 1, dtype=jnp.int32)
    spot = jax.random.randint(jax.random.fold_in(key, 1), (), 0, HQ, dtype=jnp.int32)
    index_row = jnp.arange(HQ, dtype=jnp.int32)
    counts = jnp.where(index_row == spot, SINKS, counts)
    counts = jnp.where(index_row == (spot + 1) % HQ, 1, counts)
    return counts.astype(jnp.int32)


def draw_window_len(key, part):
    key = jax.random.fold_in(key, 22)
    counts = jax.random.randint(key, (HQ,), WINDOW // 2, WINDOW + 1, dtype=jnp.int32)
    spot = jax.random.randint(jax.random.fold_in(key, 1), (), 0, HQ, dtype=jnp.int32)
    index_row = jnp.arange(HQ, dtype=jnp.int32)
    counts = jnp.where(index_row == spot, WINDOW, counts)
    counts = jnp.where(index_row == (spot + 1) % HQ, WINDOW // 2, counts)
    return counts.astype(jnp.int32)


def with_ends(values, key, low, high):
    longest = values.shape.index(max(values.shape))
    spots = []
    for shift in (0, 1):
        where = [jax.random.randint(jax.random.fold_in(key, axis), (), 0, length) for axis, length in enumerate(values.shape)]
        where[longest] = (where[longest] + shift) % values.shape[longest]
        spots.append(tuple(where))
    return values.at[spots[0]].set(low).at[spots[1]].set(high)


def block_levels(own_key, dims, split, least, largest):
    gain, own = 1.0, jax.random.fold_in(own_key, 6)
    for axis_at, parts in split:
        draws = jnp.exp(jax.random.uniform(jax.random.fold_in(own, axis_at), (parts,), jnp.float32, least / len(split), largest / len(split)))
        gain = gain * jnp.repeat(draws, dims[axis_at] // parts).reshape([-1 if axis == axis_at else 1 for axis in range(len(dims))])
    return gain


def scatter_about(key, dims, deviation, bound, shards=(), held_as=jnp.bfloat16):
    values = jax.random.normal(key, dims, jnp.float32) * deviation
    if len(shards) > 0:
        values = block_levels(key, dims, shards, -0.22, 0.18) * values
    return jnp.clip(values, min=-bound, max=bound).astype(held_as)


def setup_inputs(seed: int = 0) -> dict:
    key_list = jax.random.split(jax.random.key(seed), 9)
    queries = draw_queries(jax.random.fold_in(key_list[8], 71), 0)
    key_states = draw_key_states(jax.random.fold_in(key_list[8], 71), 0)
    value_states = scatter_about(key_list[2], (TOKENS, HK * DH), 1.0, 6.0, ((0, 32), (1, 8)))
    head_gates = jnp.clip(0.1 + 0.9 * jax.random.uniform(key_list[3], (HQ,), jnp.float32) ** block_levels(key_list[3], (HQ,), ((0, 8),), -0.2, 0.2), 0.1, 1.0)
    retrieval = with_ends((jax.random.randint(key_list[4], (HQ,), 0, 2) < 1).astype(jnp.int32), jax.random.fold_in(key_list[4], 1), 0, 1)
    sink_count = draw_sink_count(jax.random.fold_in(key_list[8], 71), 0)
    window_len = draw_window_len(jax.random.fold_in(key_list[8], 71), 0)
    out_grad = scatter_about(key_list[7], (TOKENS, HQ * DH), 1.0, 6.0, ((0, 32), (1, 8)))
    return {"queries": queries, "key_states": key_states, "value_states": value_states, "head_gates": head_gates, "retrieval": retrieval, "sink_count": sink_count, "window_len": window_len, "out_grad": out_grad}


NEGATIVE = -1e30


def reference(queries, key_states, value_states, head_gates, retrieval, sink_count, window_len, out_grad):
    group = HQ // HK
    scale = float(DH) ** -0.5
    position = jnp.arange(TOKENS, dtype=jnp.int32)
    causal = position[None, :] <= position[:, None]
    query_all = queries.reshape(TOKENS, HK, group, DH).transpose(1, 2, 0, 3)
    grad_all = out_grad.reshape(TOKENS, HK, group, DH).transpose(1, 2, 0, 3)
    key_all = key_states.reshape(TOKENS, HK, DH).transpose(1, 0, 2)
    value_all = value_states.reshape(TOKENS, HK, DH).transpose(1, 0, 2)
    gate_all = head_gates.reshape(HK, group)
    flag_all = retrieval.reshape(HK, group)
    sink_all = sink_count.reshape(HK, group)
    window_all = window_len.reshape(HK, group)

    def one_group(items):
        query_grp, grad_grp, key_head, value_head, gate_grp, flag_grp, sink_grp, window_grp = items

        def one_head(carry, head_items):
            key_sum, value_sum = carry
            query_head, grad_head, gate, flag, sink, window = head_items
            scores = jnp.dot(query_head, key_head.T, preferred_element_type=jnp.float32) * scale
            visible = causal & ((flag == 1) | (position[None, :] < sink) | (position[None, :] > position[:, None] - window))
            peak = jnp.max(jnp.where(visible, scores, NEGATIVE), axis=1)
            raised = jnp.where(visible, jnp.exp(scores - peak[:, None]), 0.0)
            total = jnp.sum(raised, axis=1)
            log_total = peak + jnp.log(total)
            weights = (raised / total[:, None]).astype(jnp.bfloat16)
            head_out = jnp.dot(weights, value_head, preferred_element_type=jnp.float32)
            attended = (gate * head_out).astype(jnp.bfloat16)
            grad_float = grad_head.astype(jnp.float32)
            products = grad_float * head_out
            gate_grad = jnp.sum(products)
            scaled_grad = (gate * grad_float).astype(jnp.bfloat16)
            delta = gate * jnp.sum(products, axis=1)
            probs = jnp.where(visible, jnp.exp(scores - log_total[:, None]), 0.0)
            grad_probs = jnp.dot(scaled_grad, value_head.T, preferred_element_type=jnp.float32)
            grad_scores = (probs * (grad_probs - delta[:, None])).astype(jnp.bfloat16)
            query_grad = (jnp.dot(grad_scores, key_head, preferred_element_type=jnp.float32) * scale).astype(jnp.bfloat16)
            key_sum = key_sum + jnp.dot(grad_scores.T, query_head, preferred_element_type=jnp.float32) * scale
            value_sum = value_sum + jnp.dot(probs.astype(jnp.bfloat16).T, scaled_grad, preferred_element_type=jnp.float32)
            return (key_sum, value_sum), (attended, query_grad, gate_grad)

        empty = jnp.zeros((TOKENS, DH), jnp.float32)
        sums, results = lax.scan(one_head, (empty, empty), (query_grp, grad_grp, gate_grp, flag_grp, sink_grp, window_grp))
        return results[0], results[1], results[2], sums[0].astype(jnp.bfloat16), sums[1].astype(jnp.bfloat16)

    attended, query_grads, gate_grads, key_grads, value_grads = lax.map(
        one_group, (query_all, grad_all, key_all, value_all, gate_all, flag_all, sink_all, window_all))
    attended = attended.transpose(2, 0, 1, 3).reshape(TOKENS, HQ * DH)
    grad_queries = query_grads.transpose(2, 0, 1, 3).reshape(TOKENS, HQ * DH)
    grad_keys = key_grads.transpose(1, 0, 2).reshape(TOKENS, HK * DH)
    grad_values = value_grads.transpose(1, 0, 2).reshape(TOKENS, HK * DH)
    grad_gates = gate_grads.reshape(HQ)
    return (attended, grad_queries, grad_keys, grad_values, grad_gates)
```

```python
import math

import jax
import jax.numpy as jnp
from jax import lax
from jax.experimental import pallas as pl
from jax.experimental.pallas import tpu as pltpu
from jax.sharding import PartitionSpec as P

DH = 128
GROUP = 8
ROWS = 192
SEG = 96
STACK = GROUP * SEG
TOKENS = 6144
WIDTH = GROUP * DH
NX = 4
NY = 4
NZ = 8
CTX = NX * NY * 2
BK = 768
SLOTS = TOKENS // BK + 1
RC = 384
NEGATIVE = -1e30
SCALE = DH**-0.5
LOGSCALE = SCALE * math.log2(math.e)
F32 = jnp.float32
BF = jnp.bfloat16
MESH = pl.DeviceIdType.MESH


def dot(a, b, ca, cb):
    return lax.dot_general(a, b, (((ca,), (cb,)), ((), ())), preferred_element_type=F32)


def ctx_of(x, y, c):
    return x * (2 * NY) + y * 2 + c


def loop(count, body):
    def step(n, carry):
        body(n)
        return carry

    lax.fori_loop(0, count, step, 0)


def train_kernel(
    flag_ref, sink_ref, win_ref, gate_ref, q_ref, g_ref, k_ref, v_ref,
    att_out, dq_out, dk_out, dv_out, gg_out,
    k_all, v_all, q_in, g_in, q_s, qt_s, g_s, gt_s, early_s, far_s, late_s, m_s, o_s, d_s, dq_s, s_s, p_s, dkt_s, dvt_s,
    att_s, dqb_s, gg_s, dk_part, dv_part, core_in, kline_in, kline_out, kline_own, klast_in, klast_out,
    vline_in, vline_out, vline_own, vlast_in, vlast_out, gate_in, gate_all,
    own, send_one, recv_one, send_two, recv_two, send_core, recv_core, send_rows, recv_rows,
    send_back, recv_back, send_pair, recv_pair, send_line, recv_line, send_vline, recv_vline,
    send_last, recv_last, send_gate, recv_gate,
):
    me = lax.axis_index("ctx")
    z = lax.axis_index("head")
    x, y, c = me // (2 * NY), (me // 2) % NY, me % 2
    other = {"ctx": ctx_of(x, y, 1 - c)}
    mirror = {"ctx": CTX - 1 - me}
    start0 = me * ROWS
    start1 = (CTX - 1 - me) * ROWS + SEG
    nb0 = start0 // BK + 1
    nb1 = start1 // BK + 1

    def across(d):
        return {"ctx": ctx_of((x + d + 1) % NX, y, c)}

    def along(d):
        return {"ctx": ctx_of(x, (y + d + 1) % NY, c)}

    def heads(d):
        return {"head": (z + d + 1) % NZ}

    def remote(src, dst, send, recv, device):
        return pltpu.make_async_remote_copy(
            src_ref=src, dst_ref=dst, send_sem=send, recv_sem=recv, device_id=device, device_id_type=MESH
        )

    def one_k(d):
        return remote(k_ref, k_all.at[x, y, c], send_one.at[0, d], recv_one.at[0, d], along(d))

    def one_v(d):
        return remote(v_ref, v_all.at[x, y, c], send_one.at[1, d], recv_one.at[1, d], across(d))

    def two_k(d):
        return remote(k_all.at[x, :, c], k_all.at[x, :, c], send_two.at[0, d], recv_two.at[0, d], across(d))

    def two_v(d):
        return remote(v_all.at[:, y, c], v_all.at[:, y, c], send_two.at[1, d], recv_two.at[1, d], along(d))

    def core_k(d):
        at = k_all.at[(x + NX - d) % NX, :, c]
        return remote(at, at, send_core.at[0, d], recv_core.at[0, d], other)

    def core_v(d):
        at = v_all.at[:, (y + NY - d) % NY, c]
        return remote(at, at, send_core.at[1, d], recv_core.at[1, d], other)

    rows_q = remote(q_ref.at[pl.ds(SEG, SEG)], q_in.at[1], send_rows.at[0], recv_rows.at[0], mirror)
    rows_g = remote(g_ref.at[pl.ds(SEG, SEG)], g_in.at[1], send_rows.at[1], recv_rows.at[1], mirror)
    back_att = remote(att_s.at[1], att_out.at[pl.ds(SEG, SEG)], send_back.at[0], recv_back.at[0], mirror)
    back_dq = remote(dqb_s.at[1], dq_out.at[pl.ds(SEG, SEG)], send_back.at[1], recv_back.at[1], mirror)

    def pair_k(n):
        return remote(dk_part.at[(x + n) % NX, :, 1 - c], core_in.at[0, n], send_pair.at[0, n], recv_pair.at[0, n], other)

    def pair_v(n):
        return remote(dv_part.at[(x + n) % NX, :, 1 - c], core_in.at[1, n], send_pair.at[1, n], recv_pair.at[1, n], other)

    def line_k(n):
        return remote(kline_out.at[n - 1], kline_in.at[n - 1], send_line.at[n - 1], recv_line.at[n - 1], across(n - 1))

    def line_v(n, e):
        return remote(vline_out.at[n, e], vline_in.at[n, e], send_vline.at[n, e], recv_vline.at[n, e], along(e))

    def last_k(e):
        return remote(klast_out.at[(y + e + 1) % NY], klast_in.at[e], send_last.at[0, e], recv_last.at[0, e], along(e))

    def last_v(n):
        return remote(vlast_out.at[n - 1], vlast_in.at[n - 1], send_last.at[1, n - 1], recv_last.at[1, n - 1], across(n - 1))

    def gate_copy(n, src, device):
        return remote(src, gate_in.at[n], send_gate.at[n], recv_gate.at[n], device)

    gate_core = gate_copy(0, gg_s, other)
    gate_across = [gate_copy(1 + d, gate_all.at[0], across(d)) for d in range(3)]
    gate_along = [gate_copy(4 + d, gate_all.at[1], along(d)) for d in range(3)]
    gate_heads = [
        remote(gate_all.at[2], gg_out.at[z], send_gate.at[7 + d], recv_gate.at[7 + d], heads(d)) for d in range(NZ - 1)
    ]

    mine = [
        pltpu.make_async_copy(k_ref, k_all.at[x, y, c], own.at[0]),
        pltpu.make_async_copy(v_ref, v_all.at[x, y, c], own.at[1]),
        pltpu.make_async_copy(q_ref.at[pl.ds(0, SEG)], q_in.at[0], own.at[2]),
        pltpu.make_async_copy(g_ref.at[pl.ds(0, SEG)], g_in.at[0], own.at[3]),
    ]
    for copy in mine:
        copy.start()
    greeted = [across(d) for d in range(3)] + [along(d) for d in range(3)] + [other, mirror]
    greeted = greeted + [heads(d) for d in range(NZ - 1)]
    barrier = pltpu.get_barrier_semaphore()
    for device in greeted:
        pl.semaphore_signal(barrier, inc=1, device_id=device, device_id_type=MESH)
    pl.semaphore_wait(barrier, len(greeted))
    for d in range(3):
        one_k(d).start()
        one_v(d).start()

    lane = lax.broadcasted_iota(jnp.int32, (SEG, DH), 1)
    row = lax.broadcasted_iota(jnp.int32, (SEG, DH), 0)

    def prepare(seg):
        start = jnp.where(seg == 0, start0, start1)
        for h in range(GROUP):
            rows = slice(h * SEG, (h + 1) * SEG)
            q_s[seg, rows, :] = q_in[seg, :, h * DH : (h + 1) * DH]
            limit = jnp.where(flag_ref[h] == 1, -1, row + start - win_ref[h])
            far_s[rows, :] = lane - limit
            early_s[rows, :] = lane - sink_ref[h]
            late_s[rows, :] = lane - row - start
        m_s[seg] = jnp.full((STACK, DH), NEGATIVE, F32)
        qt_s[seg] = q_s[seg].T

    def scores(seg, b):
        slot = b + seg * nb0
        last = jnp.where(seg == 0, nb0, nb1) - 1
        base = b * BK
        kb = k_all[b // 2, pl.ds((b % 2) * 2, 2)].reshape(BK, DH)

        def go(full):
            for r in range(0, STACK, RC):
                rows = slice(r, r + RC)
                s = dot(q_s[seg, rows, :], kb, 1, 1)
                best = m_s[seg, rows, :]
                far = far_s[rows, :]
                for t in range(BK // DH):
                    at = base + t * DH
                    seen = far > -at
                    if full:
                        seen = (seen | (early_s[rows, :] < -at)) & (late_s[rows, :] <= -at)
                    part = jnp.where(seen, s[:, t * DH : (t + 1) * DH], NEGATIVE)
                    s_s[slot, rows, t * DH : (t + 1) * DH] = part
                    best = jnp.maximum(best, part)
                m_s[seg, rows, :] = best

        edge = (b == 0) | (b == last)
        pl.when(edge)(lambda: go(True))
        pl.when(jnp.logical_not(edge))(lambda: go(False))

    mine[2].wait()
    mine[0].wait()
    mine[1].wait()
    for d in range(3):
        one_k(d).wait_recv()
        one_v(d).wait_recv()
    for d in range(3):
        two_k(d).start()
        two_v(d).start()
    core_k(0).start()
    core_v(0).start()
    rows_q.start()

    def score_step(step):
        seg = step // 4
        d = step % 4

        @pl.when((step > 0) & (step < 4))
        def _():
            two_k(d - 1).wait_recv()
            core_k(d).start()
            two_v(d - 1).wait_recv()
            core_v(d).start()

        @pl.when(step < 4)
        def _():
            core_k(d).wait_recv()

        @pl.when(step == 4)
        def _():
            rows_q.wait_recv()
            rows_g.start()

        @pl.when(d == 0)
        def _():
            prepare(seg)

        def block(t):
            b = ((x + NX - d) % NX) * 2 + t
            pl.when(b < jnp.where(seg == 0, nb0, nb1))(lambda: scores(seg, b))

        loop(2, block)

    loop(8, score_step)

    def settle(seg):
        peak = jnp.max(m_s[seg], axis=1, keepdims=True)
        m_s[seg] = jnp.broadcast_to(peak * LOGSCALE, (STACK, DH))
        o_s[seg] = jnp.zeros((STACK, 2 * DH), F32)

    loop(2, settle)
    loop(4, lambda d: core_v(d).wait_recv())

    def forward(slot):
        seg = jnp.where(slot < nb0, 0, 1)
        b = slot - seg * nb0
        vb = v_all[b // 2, pl.ds((b % 2) * 2, 2)].reshape(BK, DH)
        vx = jnp.concatenate([vb, jnp.ones((BK, DH), BF)], axis=1)
        for r in range(0, STACK, RC):
            rows = slice(r, r + RC)
            top = m_s[seg, rows, :]
            parts = []
            for t in range(BK // DH):
                part = jnp.exp2(s_s[slot, rows, t * DH : (t + 1) * DH] * LOGSCALE - top).astype(BF)
                p_s[slot, rows, t * DH : (t + 1) * DH] = part
                parts.append(part)
            o_s[seg, rows, :] += dot(jnp.concatenate(parts, axis=1), vx, 1, 0)

    loop(SLOTS, forward)

    mine[3].wait()
    rows_g.wait_recv()
    gg_s[...] = jnp.zeros((GROUP, DH), F32)

    def combine(seg):
        for h in range(GROUP):
            rows = slice(h * SEG, (h + 1) * SEG)
            columns = slice(h * DH, (h + 1) * DH)
            share = 1.0 / o_s[seg, rows, DH:]
            out = o_s[seg, rows, :DH] * share
            att_s[seg, :, columns] = (gate_ref[h] * out).astype(BF)
            grad = g_in[seg, :, columns].astype(F32)
            by_row = jnp.sum(grad * out, axis=1, keepdims=True)
            gg_s[h : h + 1, :] += jnp.broadcast_to(jnp.sum(by_row, axis=0, keepdims=True), (1, DH))
            weight = gate_ref[h] * share
            d_s[seg, rows, :] = by_row * weight
            g_s[seg, rows, :] = (grad * weight).astype(BF)
        gt_s[seg] = g_s[seg].T
        dq_s[seg] = jnp.zeros((STACK, DH), F32)

    loop(2, combine)
    keep_att = pltpu.make_async_copy(att_s.at[0], att_out.at[pl.ds(0, SEG)], own.at[4])
    keep_dq = pltpu.make_async_copy(dqb_s.at[0], dq_out.at[pl.ds(0, SEG)], own.at[5])
    keep_att.start()
    back_att.start()
    gate_core.start()

    def backward(seg, b, t):
        slot = b + seg * nb0
        kb = k_all[b // 2, pl.ds(t * 2, 2)].reshape(BK, DH)
        vb = v_all[b // 2, pl.ds(t * 2, 2)].reshape(BK, DH)
        dp = dot(g_s[seg], vb, 1, 1)
        delta = d_s[seg]
        p = p_s[slot]
        ds = jnp.concatenate(
            [p[:, i : i + DH] * (dp[:, i : i + DH] - delta).astype(BF) for i in range(0, BK, DH)], axis=1
        )
        dq_s[seg] += dot(ds, kb, 1, 0)
        dkt_s[t] += dot(qt_s[seg], ds, 1, 0)
        dvt_s[t] += dot(gt_s[seg], p, 1, 0)

    def write_dq(seg):
        for h in range(GROUP):
            dqb_s[seg, :, h * DH : (h + 1) * DH] = (dq_s[seg, h * SEG : (h + 1) * SEG, :] * SCALE).astype(BF)

    def spread_v(n):
        at = (x + n) % NX
        vline_own[n] = dv_part[at, y, c].astype(F32) + core_in[1, n, y].astype(F32)
        for e in range(3):
            to = (y + e + 1) % NY
            vline_out[n, e] = (dv_part[at, to, c].astype(F32) + core_in[1, n, to].astype(F32)).astype(BF)
            line_v(n, e).start()

    def sum_v(n):
        for e in range(3):
            line_v(n, e).wait_recv()
        total = vline_own[n]
        for e in range(3):
            total = total + vline_in[n, e].astype(F32)
        return total

    def gate_step(step):
        @pl.when(step == 0)
        def _():
            gate_core.wait_recv()
            gate_all[0] = gg_s[...] + gate_in[0]
            for copy in gate_across:
                copy.start()

        @pl.when(step == 1)
        def _():
            for copy in gate_across:
                copy.wait_recv()
            gate_all[1] = gate_all[0] + gate_in[1] + gate_in[2] + gate_in[3]
            for copy in gate_along:
                copy.start()

        @pl.when(step == 2)
        def _():
            for copy in gate_along:
                copy.wait_recv()
            total = gate_all[1] + gate_in[4] + gate_in[5] + gate_in[6]
            gate_all[2] = total
            gg_out[z] = total
            for copy in gate_heads:
                copy.start()

    def grad_step(step):
        n = (step + 1) % NX
        at = (x + n) % NX
        dkt_s[...] = jnp.zeros((2, DH, BK), F32)
        dvt_s[...] = jnp.zeros((2, DH, BK), F32)

        def turn(index):
            seg = 1 - index

            def block(t):
                b = at * 2 + t
                pl.when(b < jnp.where(seg == 0, nb0, nb1))(lambda: backward(seg, b, t))

            loop(2, block)

            @pl.when((step == 3) & (index == 0))
            def _():
                write_dq(1)
                back_dq.start()

        loop(2, turn)
        for t in range(2):
            dk_part[at, t * 2 : t * 2 + 2] = (dkt_s[t] * SCALE).T.astype(BF).reshape(2, 2, ROWS, DH)
            dv_part[at, t * 2 : t * 2 + 2] = dvt_s[t].T.astype(BF).reshape(2, 2, ROWS, DH)
        pair_k(n).start()
        pair_v(n).start()
        gate_step(step)

        @pl.when(step > 0)
        def _():
            pair_k(step).wait_recv()
            group = (x + step) % NX
            kline_out[step - 1] = (dk_part[group, :, c].astype(F32) + core_in[0, step].astype(F32)).astype(BF)
            line_k(step).start()
            pair_v(step).wait_recv()
            spread_v(step)

        @pl.when(step > 1)
        def _():
            vlast_out[step - 2] = sum_v(step - 1).astype(BF)
            last_v(step - 1).start()

    loop(4, grad_step)
    write_dq(0)
    keep_dq.start()

    pair_v(0).wait_recv()
    spread_v(0)
    pair_k(0).wait_recv()
    kline_own[...] = dk_part[x, :, c].astype(F32) + core_in[0, 0].astype(F32)
    for n in range(1, 4):
        line_k(n).wait_recv()
    kline_own[...] += kline_in[0].astype(F32) + kline_in[1].astype(F32) + kline_in[2].astype(F32)
    klast_out[...] = kline_own[...].astype(BF)
    for e in range(3):
        last_k(e).start()
    vlast_out[2] = sum_v(3).astype(BF)
    last_v(3).start()
    v_total = sum_v(0)
    k_total = kline_own[y]
    for e in range(3):
        last_k(e).wait_recv()
        k_total = k_total + klast_in[e].astype(F32)
    dk_out[...] = k_total.astype(BF)
    for n in range(1, 4):
        last_v(n).wait_recv()
        v_total = v_total + vlast_in[n - 1].astype(F32)
    dv_out[...] = v_total.astype(BF)
    for copy in gate_heads:
        copy.wait_recv()
    keep_att.wait()
    keep_dq.wait()
    back_att.wait()
    back_dq.wait()
    rows_q.wait_send()
    rows_g.wait_send()
    for d in range(3):
        one_k(d).wait_send()
        one_v(d).wait_send()
        two_k(d).wait_send()
        two_v(d).wait_send()
        line_k(d + 1).wait_send()
        last_k(d).wait_send()
        last_v(d + 1).wait_send()
    for n in range(4):
        core_k(n).wait_send()
        core_v(n).wait_send()
        pair_k(n).wait_send()
        pair_v(n).wait_send()
        for e in range(3):
            line_v(n, e).wait_send()
    for copy in [gate_core] + gate_across + gate_along + gate_heads:
        copy.wait_send()


def train(flags, sinks, wins, gates, q, g, k, v):
    smem = pl.BlockSpec(memory_space=pltpu.SMEM)
    vmem = pl.BlockSpec(memory_space=pltpu.VMEM)
    anywhere = pl.BlockSpec(memory_space=pl.ANY)
    dma = pltpu.SemaphoreType.DMA
    shape = jax.ShapeDtypeStruct
    hold = pltpu.VMEM
    whole = (NX, NY, 2, ROWS, DH)
    block = (NY, ROWS, DH)
    return pl.pallas_call(
        train_kernel,
        out_shape=(
            shape((ROWS, WIDTH), BF), shape((ROWS, WIDTH), BF), shape((ROWS, DH), BF), shape((ROWS, DH), BF),
            shape((NZ, GROUP, DH), F32),
        ),
        in_specs=[smem] * 4 + [anywhere] * 4,
        out_specs=[anywhere] * 2 + [vmem] * 3,
        scratch_shapes=[
            hold(whole, BF), hold(whole, BF), hold((2, SEG, WIDTH), BF), hold((2, SEG, WIDTH), BF),
            hold((2, STACK, DH), BF), hold((2, DH, STACK), BF), hold((2, STACK, DH), BF), hold((2, DH, STACK), BF),
            hold((STACK, DH), jnp.int32), hold((STACK, DH), jnp.int32), hold((STACK, DH), jnp.int32),
            hold((2, STACK, DH), F32), hold((2, STACK, 2 * DH), F32), hold((2, STACK, DH), F32), hold((2, STACK, DH), F32),
            hold((SLOTS, STACK, BK), F32), hold((SLOTS, STACK, BK), BF), hold((2, DH, BK), F32), hold((2, DH, BK), F32),
            hold((2, SEG, WIDTH), BF), hold((2, SEG, WIDTH), BF), hold((GROUP, DH), F32),
            hold(whole, BF), hold(whole, BF), hold((2, 4) + block, BF),
            hold((3,) + block, BF), hold((3,) + block, BF), hold(block, F32), hold((3, ROWS, DH), BF), hold(block, BF),
            hold((4, 3, ROWS, DH), BF), hold((4, 3, ROWS, DH), BF), hold((4, ROWS, DH), F32),
            hold((3, ROWS, DH), BF), hold((3, ROWS, DH), BF),
            hold((7, GROUP, DH), F32), hold((3, GROUP, DH), F32),
            dma((6,)), dma((2, 3)), dma((2, 3)), dma((2, 3)), dma((2, 3)), dma((2, 4)), dma((2, 4)), dma((2,)), dma((2,)),
            dma((2,)), dma((2,)), dma((2, 4)), dma((2, 4)), dma((3,)), dma((3,)), dma((4, 3)), dma((4, 3)),
            dma((2, 3)), dma((2, 3)), dma((14,)), dma((14,)),
        ],
        compiler_params=pltpu.CompilerParams(
            collective_id=0, has_side_effects=True, vmem_limit_bytes=60 * 1024 * 1024
        ),
        name="train",
    )(flags, sinks, wins, gates, q, g, k, v)


def local(queries, key_states, value_states, head_gates, retrieval, sink_count, window_len, out_grad):
    att, dq, dk, dv, gg = train(
        retrieval, sink_count, window_len, head_gates, queries, out_grad, key_states, value_states
    )
    return att, dq, dk, dv, gg[:, :, 0].reshape(NZ * GROUP)


def solution(mesh):
    wide = P("ctx", "head")
    return jax.shard_map(
        local,
        mesh=mesh,
        in_specs=(wide, wide, wide, P("head"), P("head"), P("head"), P("head"), wide),
        out_specs=(wide, wide, wide, wide, P()),
        check_vma=False,
    )
```

```python
import math

import jax
import jax.numpy as jnp
from jax import lax
from jax.experimental import pallas as pl
from jax.experimental.pallas import tpu as pltpu
from jax.sharding import PartitionSpec as P

DH = 128
GROUP = 8
ROWS = 192
MOVE = 48
SEGS = (ROWS - MOVE, MOVE)
STACKS = (GROUP * SEGS[0], GROUP * SEGS[1])
UNIT = GROUP * MOVE
UNITS = tuple(n // UNIT for n in STACKS)
TOKENS = 6144
WIDTH = GROUP * DH
NX = 4
NY = 4
NZ = 8
CTX = NX * NY * 2
BK = 768
BLOCKS = TOKENS // BK
SLOTS = BLOCKS * UNITS[0] + UNITS[1]
NEGATIVE = -1e30
SCALE = DH**-0.5
LOGSCALE = SCALE * math.log2(math.e)
F32 = jnp.float32
BF = jnp.bfloat16
MESH = pl.DeviceIdType.MESH


def dot(a, b, ca, cb):
    return lax.dot_general(a, b, (((ca,), (cb,)), ((), ())), preferred_element_type=F32)


def ctx_of(x, y, c):
    return x * (2 * NY) + y * 2 + c


def loop(count, body):
    def step(n, carry):
        body(n)
        return carry

    lax.fori_loop(0, count, step, 0)


def train_kernel(
    flag_ref, sink_ref, win_ref, gate_ref, q_ref, g_ref, k_ref, v_ref,
    att_out, dq_out, dk_out, dv_out, gg_out,
    k_all, v_all, q_in0, q_in1, g_in0, g_in1, q_s0, q_s1, qt_s0, qt_s1, g_s0, g_s1, gt_s0, gt_s1,
    early_s0, early_s1, far_s0, far_s1, late_s0, late_s1, m_s0, m_s1, o_s0, o_s1, d_s0, d_s1, dq_s0, dq_s1, s_s, dkt_s, dvt_s,
    att_s0, att_s1, dqb_s0, dqb_s1, gg_s, dk_part, dv_part, core_in, kline_in, kline_out, kline_own, klast_in, klast_out,
    vline_in, vline_out, vline_own, vlast_in, vlast_out, gate_in, gate_all,
    own, send_one, recv_one, send_two, recv_two, send_core, recv_core, send_rows, recv_rows,
    send_back, recv_back, send_pair, recv_pair, send_line, recv_line, send_vline, recv_vline,
    send_last, recv_last, send_gate, recv_gate,
):
    q_in, g_in, q_s, qt_s, g_s, gt_s = (q_in0, q_in1), (g_in0, g_in1), (q_s0, q_s1), (qt_s0, qt_s1), (g_s0, g_s1), (gt_s0, gt_s1)
    early_s, far_s, late_s = (early_s0, early_s1), (far_s0, far_s1), (late_s0, late_s1)
    m_s, o_s, d_s, dq_s, att_s, dqb_s = (m_s0, m_s1), (o_s0, o_s1), (d_s0, d_s1), (dq_s0, dq_s1), (att_s0, att_s1), (dqb_s0, dqb_s1)
    me = lax.axis_index("ctx")
    z = lax.axis_index("head")
    x, y, c = me // (2 * NY), (me // 2) % NY, me % 2
    other = {"ctx": ctx_of(x, y, 1 - c)}
    mirror = {"ctx": CTX - 1 - me}
    start0 = me * ROWS
    start1 = (CTX - 1 - me) * ROWS + SEGS[0]
    nb0 = start0 // BK + 1
    nb1 = start1 // BK + 1
    starts = (start0, start1)
    blocks = (nb0, nb1)
    bases = (0, nb0 * UNITS[0])

    def across(d):
        return {"ctx": ctx_of((x + d + 1) % NX, y, c)}

    def along(d):
        return {"ctx": ctx_of(x, (y + d + 1) % NY, c)}

    def heads(d):
        return {"head": (z + d + 1) % NZ}

    def remote(src, dst, send, recv, device):
        return pltpu.make_async_remote_copy(
            src_ref=src, dst_ref=dst, send_sem=send, recv_sem=recv, device_id=device, device_id_type=MESH
        )

    def one_k(d):
        return remote(k_ref, k_all.at[x, y, c], send_one.at[0, d], recv_one.at[0, d], along(d))

    def one_v(d):
        return remote(v_ref, v_all.at[x, y, c], send_one.at[1, d], recv_one.at[1, d], across(d))

    def two_k(d, j):
        at = k_all.at[x, (y + NY - j) % NY, c]
        return remote(at, at, send_two.at[0, d, j], recv_two.at[0, d, j], across(d))

    def two_v(d, j):
        at = v_all.at[(x + NX - j) % NX, y, c]
        return remote(at, at, send_two.at[1, d, j], recv_two.at[1, d, j], along(d))

    def core_k(d):
        at = k_all.at[(x + NX - d) % NX, :, c]
        return remote(at, at, send_core.at[0, d], recv_core.at[0, d], other)

    def core_v(d):
        at = v_all.at[:, (y + NY - d) % NY, c]
        return remote(at, at, send_core.at[1, d], recv_core.at[1, d], other)

    rows_q = remote(q_ref.at[pl.ds(SEGS[0], MOVE)], q_in[1], send_rows.at[0], recv_rows.at[0], mirror)
    rows_g = remote(g_ref.at[pl.ds(SEGS[0], MOVE)], g_in[1], send_rows.at[1], recv_rows.at[1], mirror)
    back_att = remote(att_s[1], att_out.at[pl.ds(SEGS[0], MOVE)], send_back.at[0], recv_back.at[0], mirror)
    back_dq = remote(dqb_s[1], dq_out.at[pl.ds(SEGS[0], MOVE)], send_back.at[1], recv_back.at[1], mirror)

    def pair_k(n):
        return remote(dk_part.at[(x + n) % NX, :, 1 - c], core_in.at[0, n], send_pair.at[0, n], recv_pair.at[0, n], other)

    def pair_v(n):
        return remote(dv_part.at[(x + n) % NX, :, 1 - c], core_in.at[1, n], send_pair.at[1, n], recv_pair.at[1, n], other)

    def line_k(n):
        return remote(kline_out.at[n - 1], kline_in.at[n - 1], send_line.at[n - 1], recv_line.at[n - 1], across(n - 1))

    def line_v(n, e):
        return remote(vline_out.at[n, e], vline_in.at[n, e], send_vline.at[n, e], recv_vline.at[n, e], along(e))

    def last_k(e):
        return remote(klast_out.at[(y + e + 1) % NY], klast_in.at[e], send_last.at[0, e], recv_last.at[0, e], along(e))

    def last_v(n):
        return remote(vlast_out.at[n - 1], vlast_in.at[n - 1], send_last.at[1, n - 1], recv_last.at[1, n - 1], across(n - 1))

    def gate_copy(n, src, device):
        return remote(src, gate_in.at[n], send_gate.at[n], recv_gate.at[n], device)

    gate_core = gate_copy(0, gg_s, other)
    gate_across = [gate_copy(1 + d, gate_all.at[0], across(d)) for d in range(3)]
    gate_along = [gate_copy(4 + d, gate_all.at[1], along(d)) for d in range(3)]
    gate_heads = [
        remote(gate_all.at[2], gate_in.at[7 + d], send_gate.at[7 + d], recv_gate.at[7 + d], heads(d)) for d in range(NZ - 1)
    ]

    mine = [
        pltpu.make_async_copy(k_ref, k_all.at[x, y, c], own.at[0]),
        pltpu.make_async_copy(v_ref, v_all.at[x, y, c], own.at[1]),
        pltpu.make_async_copy(q_ref.at[pl.ds(0, SEGS[0])], q_in[0], own.at[2]),
        pltpu.make_async_copy(g_ref.at[pl.ds(0, SEGS[0])], g_in[0], own.at[3]),
    ]
    for copy in mine:
        copy.start()
    greeted = [across(d) for d in range(3)] + [along(d) for d in range(3)] + [other, mirror]
    greeted = greeted + [heads(d) for d in range(NZ - 1)]
    barrier = pltpu.get_barrier_semaphore()
    for device in greeted:
        pl.semaphore_signal(barrier, inc=1, device_id=device, device_id_type=MESH)
    pl.semaphore_wait(barrier, len(greeted))
    for d in range(3):
        one_k(d).start()
        one_v(d).start()
    mine[0].wait()
    mine[1].wait()
    for d in range(3):
        two_k(d, 0).start()
        two_v(d, 0).start()

    def prepare(seg):
        size = SEGS[seg]
        lane = lax.broadcasted_iota(jnp.int32, (size, DH), 1)
        row = lax.broadcasted_iota(jnp.int32, (size, DH), 0)
        for h in range(GROUP):
            rows = slice(h * size, (h + 1) * size)
            q_s[seg][rows, :] = q_in[seg][:, h * DH : (h + 1) * DH]
            limit = jnp.where(flag_ref[h] == 1, -1, row + starts[seg] - win_ref[h])
            far_s[seg][rows, :] = lane - limit
            early_s[seg][rows, :] = lane - sink_ref[h]
            late_s[seg][rows, :] = lane - row - starts[seg]
        m_s[seg][...] = jnp.full((STACKS[seg], DH), NEGATIVE, F32)
        qt_s[seg][...] = q_s[seg][...].T

    def scores(seg, b):
        base = b * BK
        kb = k_all[b // 2, pl.ds((b % 2) * 2, 2)].reshape(BK, DH)

        def go(full):
            for u in range(UNITS[seg]):
                rows = slice(u * UNIT, (u + 1) * UNIT)
                slot = bases[seg] + b * UNITS[seg] + u
                s = dot(q_s[seg][rows, :], kb, 1, 1)
                best = m_s[seg][rows, :]
                far = far_s[seg][rows, :]
                for t in range(BK // DH):
                    at = base + t * DH
                    seen = far > -at
                    if full:
                        seen = (seen | (early_s[seg][rows, :] < -at)) & (late_s[seg][rows, :] <= -at)
                    part = jnp.where(seen, s[:, t * DH : (t + 1) * DH], NEGATIVE)
                    s_s[slot, :, t * DH : (t + 1) * DH] = part
                    best = jnp.maximum(best, part)
                m_s[seg][rows, :] = best

        edge = (b == 0) | (b == blocks[seg] - 1)
        pl.when(edge)(lambda: go(True))
        pl.when(jnp.logical_not(edge))(lambda: go(False))

    for j in range(1, 4):
        one_k(j - 1).wait_recv()
        one_v(j - 1).wait_recv()
        for d in range(3):
            two_k(d, j).start()
            two_v(d, j).start()
    mine[2].wait()
    core_k(0).start()
    core_v(0).start()
    rows_q.start()

    prepare(0)

    def score_step(d):
        @pl.when(d > 0)
        def _():
            for j in range(4):
                two_k(d - 1, j).wait_recv()
            core_k(d).start()
            for j in range(4):
                two_v(d - 1, j).wait_recv()
            core_v(d).start()

        core_k(d).wait_recv()

        def block(t):
            b = ((x + NX - d) % NX) * 2 + t
            pl.when(b < nb0)(lambda: scores(0, b))

        loop(2, block)

    loop(4, score_step)
    rows_q.wait_recv()
    rows_g.start()
    prepare(1)
    loop(nb1, lambda b: scores(1, b))
    for seg in range(2):
        peak = jnp.max(m_s[seg][...], axis=1, keepdims=True)
        m_s[seg][...] = jnp.broadcast_to(peak * LOGSCALE, (STACKS[seg], DH))
        o_s[seg][...] = jnp.zeros((STACKS[seg], 2 * DH), F32)
    loop(4, lambda d: core_v(d).wait_recv())

    def forward(seg, b):
        vb = v_all[b // 2, pl.ds((b % 2) * 2, 2)].reshape(BK, DH)
        vx = jnp.concatenate([vb, jnp.ones((BK, DH), BF)], axis=1)
        for u in range(UNITS[seg]):
            rows = slice(u * UNIT, (u + 1) * UNIT)
            slot = bases[seg] + b * UNITS[seg] + u
            top = m_s[seg][rows, :]
            parts = []
            for t in range(BK // DH):
                part = jnp.exp2(s_s[slot, :, t * DH : (t + 1) * DH] * LOGSCALE - top)
                s_s[slot, :, t * DH : (t + 1) * DH] = part
                parts.append(part.astype(BF))
            o_s[seg][rows, :] += dot(jnp.concatenate(parts, axis=1), vx, 1, 0)

    loop(nb0, lambda b: forward(0, b))
    loop(nb1, lambda b: forward(1, b))

    mine[3].wait()
    rows_g.wait_recv()
    spot = lax.broadcasted_iota(jnp.int32, (8, DH), 1) - z * GROUP
    gg_s[...] = jnp.zeros((8, DH), F32)

    for seg in range(2):
        size = SEGS[seg]
        for h in range(GROUP):
            rows = slice(h * size, (h + 1) * size)
            columns = slice(h * DH, (h + 1) * DH)
            share = 1.0 / o_s[seg][rows, DH:]
            out = o_s[seg][rows, :DH] * share
            att_s[seg][:, columns] = (gate_ref[h] * out).astype(BF)
            grad = g_in[seg][:, columns].astype(F32)
            by_row = jnp.sum(grad * out, axis=1, keepdims=True)
            gg_s[...] += jnp.where(spot == h, jnp.sum(by_row, axis=0, keepdims=True), 0.0)
            weight = gate_ref[h] * share
            d_s[seg][rows, :] = by_row * weight
            g_s[seg][rows, :] = (grad * weight).astype(BF)
        gt_s[seg][...] = g_s[seg][...].T
        dq_s[seg][...] = jnp.zeros((STACKS[seg], DH), F32)

    keep_att = pltpu.make_async_copy(att_s[0], att_out.at[pl.ds(0, SEGS[0])], own.at[4])
    keep_dq = pltpu.make_async_copy(dqb_s[0], dq_out.at[pl.ds(0, SEGS[0])], own.at[5])
    keep_att.start()
    back_att.start()
    gate_core.start()

    def backward(seg, b, t):
        kb = k_all[b // 2, pl.ds(t * 2, 2)].reshape(BK, DH)
        vb = v_all[b // 2, pl.ds(t * 2, 2)].reshape(BK, DH)
        slot = bases[seg] + b * UNITS[seg]
        dp = dot(g_s[seg][...], vb, 1, 1)
        delta = d_s[seg][...]
        p = s_s[pl.ds(slot, UNITS[seg])].reshape(STACKS[seg], BK).astype(BF)
        ds = jnp.concatenate(
            [p[:, i : i + DH] * (dp[:, i : i + DH] - delta).astype(BF) for i in range(0, BK, DH)], axis=1
        )
        dq_s[seg][...] += dot(ds, kb, 1, 0)
        dkt_s[t] += dot(qt_s[seg][...], ds, 1, 0)
        dvt_s[t] += dot(gt_s[seg][...], p, 1, 0)

    def write_dq(seg):
        size = SEGS[seg]
        for h in range(GROUP):
            dqb_s[seg][:, h * DH : (h + 1) * DH] = (dq_s[seg][h * size : (h + 1) * size, :] * SCALE).astype(BF)

    def spread_v(n):
        at = (x + n) % NX
        vline_own[n] = dv_part[at, y, c].astype(F32) + core_in[1, n, y].astype(F32)
        for e in range(3):
            to = (y + e + 1) % NY
            vline_out[n, e] = (dv_part[at, to, c].astype(F32) + core_in[1, n, to].astype(F32)).astype(BF)
            line_v(n, e).start()

    def sum_v(n):
        for e in range(3):
            line_v(n, e).wait_recv()
        total = vline_own[n]
        for e in range(3):
            total = total + vline_in[n, e].astype(F32)
        return total

    def gate_step(step):
        @pl.when(step == 0)
        def _():
            gate_core.wait_recv()
            gate_all[0] = gg_s[...] + gate_in[0]
            for copy in gate_across:
                copy.start()

        @pl.when(step == 1)
        def _():
            for copy in gate_across:
                copy.wait_recv()
            gate_all[1] = gate_all[0] + gate_in[1] + gate_in[2] + gate_in[3]
            for copy in gate_along:
                copy.start()

        @pl.when(step == 2)
        def _():
            for copy in gate_along:
                copy.wait_recv()
            total = gate_all[1] + gate_in[4] + gate_in[5] + gate_in[6]
            gate_all[2] = total
            for copy in gate_heads:
                copy.start()

    def pass_on(n):
        pair_k(n).wait_recv()
        group = (x + n) % NX
        kline_out[n - 1] = (dk_part[group, :, c].astype(F32) + core_in[0, n].astype(F32)).astype(BF)
        line_k(n).start()
        pair_v(n).wait_recv()
        spread_v(n)

    def grad_step(step):
        n = (step + 1) % NX
        at = (x + n) % NX
        dkt_s[...] = jnp.zeros((2, DH, BK), F32)
        dvt_s[...] = jnp.zeros((2, DH, BK), F32)

        for seg in (1, 0):

            def block(t):
                b = at * 2 + t
                if seg == 0:
                    pl.when((step > 0) & (t == 1))(lambda: pass_on(step))
                pl.when(b < blocks[seg])(lambda: backward(seg, b, t))

            loop(2, block)
            if seg == 1:

                @pl.when(step == 3)
                def _():
                    write_dq(1)
                    back_dq.start()

        for t in range(2):
            dk_part[at, t * 2 : t * 2 + 2] = (dkt_s[t] * SCALE).T.astype(BF).reshape(2, 2, ROWS, DH)
            dv_part[at, t * 2 : t * 2 + 2] = dvt_s[t].T.astype(BF).reshape(2, 2, ROWS, DH)
        pair_k(n).start()
        pair_v(n).start()
        gate_step(step)

        @pl.when(step > 1)
        def _():
            vlast_out[step - 2] = sum_v(step - 1).astype(BF)
            last_v(step - 1).start()

    loop(4, grad_step)
    write_dq(0)
    keep_dq.start()

    pair_v(0).wait_recv()
    spread_v(0)
    pair_k(0).wait_recv()
    kline_own[...] = dk_part[x, :, c].astype(F32) + core_in[0, 0].astype(F32)
    for n in range(1, 4):
        line_k(n).wait_recv()
    kline_own[...] += kline_in[0].astype(F32) + kline_in[1].astype(F32) + kline_in[2].astype(F32)
    klast_out[...] = kline_own[...].astype(BF)
    for e in range(3):
        last_k(e).start()
    vlast_out[2] = sum_v(3).astype(BF)
    last_v(3).start()
    v_total = sum_v(0)
    k_total = kline_own[y]
    for e in range(3):
        last_k(e).wait_recv()
        k_total = k_total + klast_in[e].astype(F32)
    dk_out[...] = k_total.astype(BF)
    for n in range(1, 4):
        last_v(n).wait_recv()
        v_total = v_total + vlast_in[n - 1].astype(F32)
    dv_out[...] = v_total.astype(BF)
    total = gate_all[2]
    for d in range(NZ - 1):
        gate_heads[d].wait_recv()
        total = total + gate_in[7 + d]
    gg_out[...] = total
    keep_att.wait()
    keep_dq.wait()
    back_att.wait()
    back_dq.wait()
    rows_q.wait_send()
    rows_g.wait_send()
    for d in range(3):
        one_k(d).wait_send()
        one_v(d).wait_send()
        for j in range(4):
            two_k(d, j).wait_send()
            two_v(d, j).wait_send()
        line_k(d + 1).wait_send()
        last_k(d).wait_send()
        last_v(d + 1).wait_send()
    for n in range(4):
        core_k(n).wait_send()
        core_v(n).wait_send()
        pair_k(n).wait_send()
        pair_v(n).wait_send()
        for e in range(3):
            line_v(n, e).wait_send()
    for copy in [gate_core] + gate_across + gate_along + gate_heads:
        copy.wait_send()


def train(flags, sinks, wins, gates, q, g, k, v):
    smem = pl.BlockSpec(memory_space=pltpu.SMEM)
    vmem = pl.BlockSpec(memory_space=pltpu.VMEM)
    anywhere = pl.BlockSpec(memory_space=pl.ANY)
    dma = pltpu.SemaphoreType.DMA
    shape = jax.ShapeDtypeStruct
    hold = pltpu.VMEM
    whole = (NX, NY, 2, ROWS, DH)
    block = (NY, ROWS, DH)
    return pl.pallas_call(
        train_kernel,
        out_shape=(
            shape((ROWS, WIDTH), BF), shape((ROWS, WIDTH), BF), shape((ROWS, DH), BF), shape((ROWS, DH), BF),
            shape((8, DH), F32),
        ),
        in_specs=[smem] * 4 + [anywhere] * 4,
        out_specs=[anywhere] * 2 + [vmem] * 3,
        scratch_shapes=[
            hold(whole, BF), hold(whole, BF),
            *[hold((n, WIDTH), BF) for n in SEGS * 2],
            *[hold(dims, BF) for _ in range(2) for dims in ((STACKS[0], DH), (STACKS[1], DH), (DH, STACKS[0]), (DH, STACKS[1]))],
            *[hold((n, DH), jnp.int32) for n in STACKS * 3],
            *[hold((n, wide), F32) for wide in (DH, 2 * DH, DH, DH) for n in STACKS],
            hold((SLOTS, UNIT, BK), F32), hold((2, DH, BK), F32), hold((2, DH, BK), F32),
            *[hold((n, WIDTH), BF) for n in SEGS * 2], hold((8, DH), F32),
            hold(whole, BF), hold(whole, BF), hold((2, 4) + block, BF),
            hold((3,) + block, BF), hold((3,) + block, BF), hold(block, F32), hold((3, ROWS, DH), BF), hold(block, BF),
            hold((4, 3, ROWS, DH), BF), hold((4, 3, ROWS, DH), BF), hold((4, ROWS, DH), F32),
            hold((3, ROWS, DH), BF), hold((3, ROWS, DH), BF),
            hold((14, 8, DH), F32), hold((3, 8, DH), F32),
            dma((6,)), dma((2, 3)), dma((2, 3)), dma((2, 3, 4)), dma((2, 3, 4)), dma((2, 4)), dma((2, 4)), dma((2,)), dma((2,)),
            dma((2,)), dma((2,)), dma((2, 4)), dma((2, 4)), dma((3,)), dma((3,)), dma((4, 3)), dma((4, 3)),
            dma((2, 3)), dma((2, 3)), dma((14,)), dma((14,)),
        ],
        compiler_params=pltpu.CompilerParams(
            collective_id=0, has_side_effects=True, vmem_limit_bytes=60 * 1024 * 1024
        ),
        name="train",
    )(flags, sinks, wins, gates, q, g, k, v)


def hand_kernel(att_ref, dq_ref, dk_ref, dv_ref, gg_ref, att_out, dq_out, dk_out, dv_out, gg_out, att_s, dq_s, dk_s, dv_s, sems):
    fetched = [
        pltpu.make_async_copy(src, dst, sems.at[n])
        for n, (src, dst) in enumerate(((att_ref, att_s), (dq_ref, dq_s), (dk_ref, dk_s), (dv_ref, dv_s)))
    ]
    stored = [
        pltpu.make_async_copy(src, dst, sems.at[4 + n])
        for n, (src, dst) in enumerate(((att_s, att_out), (dq_s, dq_out), (dk_s, dk_out), (dv_s, dv_out)))
    ]
    for copy in fetched:
        copy.start()
    gg_out[...] = gg_ref[0, : NZ * GROUP]
    for n in range(4):
        fetched[n].wait()
        stored[n].start()
    for copy in stored:
        copy.wait()


def hand(att, dq, dk, dv, gg):
    vmem = pl.BlockSpec(memory_space=pltpu.VMEM)
    anywhere = pl.BlockSpec(memory_space=pl.ANY)
    shape = jax.ShapeDtypeStruct
    return pl.pallas_call(
        hand_kernel,
        out_shape=(
            shape(att.shape, BF), shape(dq.shape, BF), shape(dk.shape, BF), shape(dv.shape, BF), shape((NZ * GROUP,), F32),
        ),
        in_specs=[anywhere] * 4 + [vmem],
        out_specs=[anywhere] * 4 + [vmem],
        scratch_shapes=[*[pltpu.VMEM(part.shape, BF) for part in (att, dq, dk, dv)], pltpu.SemaphoreType.DMA((8,))],
        name="hand",
    )(att, dq, dk, dv, gg)


def local(queries, key_states, value_states, head_gates, retrieval, sink_count, window_len, out_grad):
    return hand(
        *train(retrieval, sink_count, window_len, head_gates, queries, out_grad, key_states, value_states)
    )


def solution(mesh):
    wide = P("ctx", "head")
    return jax.shard_map(
        local,
        mesh=mesh,
        in_specs=(wide, wide, wide, P("head"), P("head"), P("head"), P("head"), wide),
        out_specs=(wide, wide, wide, wide, P()),
        check_vma=False,
    )
```
